32 devices in a mesh: req: 4 (over y, core), tp: 8 (over z, x).
Axes of the slice: x: 2, y: 2, z: 4, core: 2. Of those that a mesh axis runs over, the one named last changes fastest.
Arguments:
- queries: bfloat16 [16, 32, 4096], P('req'), may hold values from -128 to 128
- cache_keys: bfloat16 [16, 4096, 512], P('req', 'tp'), may hold values from -4 to 4
- cache_values: bfloat16 [16, 4096, 512], P('req', 'tp'), may hold values from -5 to 5
- tree_keys: bfloat16 [16, 32, 512], P('req', 'tp'), may hold values from -5 to 5
- tree_values: bfloat16 [16, 32, 512], P('req', 'tp'), may hold values from -5 to 5
- parents: int32 [16, 32], P('req'), may hold values from -1 to 30, as said below
- lengths: int32 [16], P('req'), may hold values from 2 to 4096
- accepted_leaf: int32 [16], P('req'), may hold values from 0 to 31
- residual: bfloat16 [16, 32, 8192], P('req', None, 'tp'), may hold values from -12 to 12
- norm_gain: float32 [8192], replicated, may hold values from 0.5 to 4
- out_weight: bfloat16 [4096, 8192], P('tp'), may hold values from -0.09375 to 0.09375
- prev_feature: bfloat16 [16, 8192], P('req'), may hold values from -5 to 5
- draft_weight: bfloat16 [8192, 8192], P('req', 'tp'), may hold values from -0.0625 to 0.0625
- first_moment: float32 [8192, 8192], P('req', 'tp'), may hold values from -5 to 5
- second_moment: float32 [8192, 8192], P('req', 'tp'), may hold values from 0.25 to 4
Outputs:
- features: bfloat16 [16, 32, 8192], P('req', None, 'tp')
- new_weight: bfloat16 [8192, 8192], P('req', 'tp')
- new_first: float32 [8192, 8192], P('req', 'tp')
- new_second: float32 [8192, 8192], P('req', 'tp')
- draft_loss: float32 [], replicated
The draws below stay inside these ranges and needn't reach their ends.
Inputs may be any that keep to these rules, and one draw needn't show every extreme that they name: parents[r, 0] = -1; for i of 1 or more, parents[r, i] lies in 0 to i - 1; node 31 is a child of node 30.
All inputs are finite; a program needn't handle non-finite values.
Results may differ from the reference program's by a relative error of at most 0.014.
Values may be sent and summed in bfloat16 or wider, within the bound.
A program may use at most 192 MiB of HBM per device.

```python
import math
import jax
import jax.numpy as jnp
from jax import lax

D = 8192
HEADS = 32
KV_HEADS = 4
HEAD = 128
NODES = 32
CACHE = 4096
REQS = 16
N_TP = 8


def anchor_keys(key):
    return jnp.clip(jax.random.normal(jax.random.fold_in(key, 7001), (REQS, KV_HEADS * HEAD), jnp.float32), -4.0, 4.0)


def draw_queries(key, part):
    groups = HEADS // KV_HEADS
    normal_part = 2.5 * jnp.clip(jax.random.normal(jax.random.fold_in(key, 1), (REQS, NODES, KV_HEADS, groups, HEAD), jnp.float32), -4.0, 4.0)
    normal_part = jnp.clip(normal_part, -128.0, 128.0)
    return normal_part.reshape(REQS, NODES, HEADS * HEAD).astype(jnp.bfloat16)


def draw_cache_keys(key, part):
    normal_part = jnp.clip(jax.random.normal(jax.random.fold_in(key, 11), (REQS, CACHE, KV_HEADS * HEAD), jnp.float32), -4.0, 4.0)
    anchor = anchor_keys(key)
    second = normal_part[:, 1, :]
    normal_part = normal_part.at[:, 0, :].set(anchor).at[:, 1, :].set(second)
    return normal_part.astype(jnp.bfloat16)


def draw_residual(key, part):
    column = jnp.arange(D, dtype=jnp.float32) / D
    column_power = 0.5 * column + 0.5 * jax.random.uniform(jax.random.fold_in(key, 21), (D,), jnp.float32)
    row_power = jax.random.uniform(jax.random.fold_in(key, 22), (REQS, NODES, 1), jnp.float32)
    scales = 0.03 * jnp.exp(math.log(10.0) * (column_power[None, None, :] + row_power))
    jitter = jnp.clip(jax.random.normal(jax.random.fold_in(key, 23), (REQS, NODES, D), jnp.float32), -4.0, 4.0)
    return (scales * jitter).astype(jnp.bfloat16)


def draw_parents(key, part):
    node_ids = jnp.arange(NODES, dtype=jnp.int32)
    upper_bound = jnp.maximum(node_ids, 1)
    picked = jax.random.randint(jax.random.fold_in(key, 31), (REQS, NODES), 0, upper_bound[None, :], dtype=jnp.int32)
    picked = jnp.where(node_ids[None, :] == NODES - 1, NODES - 2, picked)
    return jnp.where(node_ids[None, :] == 0, -1, picked).astype(jnp.int32)


def draw_lengths(key, part):
    request_ids = jnp.arange(REQS, dtype=jnp.int32)
    low_end = 2 + (CACHE - 2) * request_ids // REQS
    high_end = 2 + (CACHE - 2) * (request_ids + 1) // REQS
    picked = jax.random.randint(jax.random.fold_in(key, 41), (REQS,), low_end, high_end + 1, dtype=jnp.int32)
    picked = jnp.where(request_ids == 0, 2, picked)
    picked = jnp.where(request_ids == REQS - 1, CACHE, picked)
    return picked.astype(jnp.int32)


def draw_norm_gain(key, part):
    column = jnp.arange(D, dtype=jnp.float32) / D
    base = jnp.exp(0.5 * math.log(3.0) * column)
    jitter = jax.random.uniform(jax.random.fold_in(key, 52), (D,), jnp.float32, minval=0.7, maxval=1.3)
    return base * jitter


def place_ends(values, stream_key, least, largest):
    place = [jax.random.randint(jax.random.fold_in(stream_key, axis), (), 0, length) for axis, length in enumerate(values.shape)]
    main_axis = values.shape.index(max(values.shape))
    next_to = place[:main_axis] + [(place[main_axis] + 1) % values.shape[main_axis]] + place[main_axis + 1:]
    return values.at[tuple(place)].set(least).at[tuple(next_to)].set(largest)


def shard_levels(stream_key, dims, cuts, low, high):
    def one(axis_at, blocks):
        steps = jax.random.uniform(jax.random.fold_in(jax.random.fold_in(stream_key, 6), axis_at), (blocks,), jnp.float32, low / len(cuts), high / len(cuts))
        return jnp.repeat(jnp.exp(steps), dims[axis_at] // blocks).reshape((-1,) + (1,) * (len(dims) - axis_at - 1))

    loudness = one(*cuts[0])
    for cut in cuts[1:]:
        loudness = loudness * one(*cut)
    return loudness


def centred(key, dims, spread, most, split=(), kind=jnp.bfloat16):
    drawn = spread * jax.random.normal(key, dims, jnp.float32)
    if split:
        drawn = drawn * shard_levels(key, dims, split, -0.22, 0.18)
    return jnp.clip(drawn, -most, most).astype(kind)


def setup_inputs(seed: int = 0) -> dict:
    streams_of = jax.random.split(jax.random.key(seed), 16)
    queries = draw_queries(jax.random.fold_in(streams_of[15], 71), 0)
    cache_keys = draw_cache_keys(jax.random.fold_in(streams_of[15], 71), 0)
    cache_values = centred(streams_of[2], (REQS, CACHE, KV_HEADS * HEAD), 1.0, 5.0, ((0, 4), (1, 8)))
    tree_keys = centred(streams_of[3], (REQS, NODES, KV_HEADS * HEAD), 1.0, 5.0, ((0, 4), (1, 8)))
    tree_values = centred(streams_of[4], (REQS, NODES, KV_HEADS * HEAD), 1.0, 5.0, ((0, 4), (1, 8)))
    parents = draw_parents(jax.random.fold_in(streams_of[15], 71), 0)
    lengths = draw_lengths(jax.random.fold_in(streams_of[15], 71), 0)
    accepted_leaf = place_ends(jax.random.randint(streams_of[7], (REQS,), 0, NODES), jax.random.fold_in(streams_of[7], 1), 0, NODES - 1).astype(jnp.int32)
    residual = draw_residual(jax.random.fold_in(streams_of[15], 71), 0)
    norm_gain = draw_norm_gain(jax.random.fold_in(streams_of[15], 71), 0)
    out_weight = centred(streams_of[10], (HEADS * HEAD, D), (HEADS * HEAD) ** -0.5, 0.09375, ((0, 8),))
    prev_feature = centred(streams_of[11], (REQS, D), 1.0, 5.0, ((0, 4),))
    draft_weight = centred(streams_of[12], (D, D), D ** -0.5, 0.0625, ((0, 4), (1, 8)))
    first_moment = centred(streams_of[13], (D, D), 1.0, 5.0, ((0, 4), (1, 8)), jnp.float32)
    second_moment = jnp.clip(jnp.exp(math.log(4.0) - 2.7725887 * jax.random.uniform(streams_of[14], (D, D), jnp.float32) ** shard_levels(streams_of[14], (D, D), ((0, 4), (1, 8)), -0.2, 0.2)), 0.25, 4.0)
    return {"queries": queries, "cache_keys": cache_keys, "cache_values": cache_values, "tree_keys": tree_keys, "tree_values": tree_values, "parents": parents, "lengths": lengths, "accepted_leaf": accepted_leaf, "residual": residual, "norm_gain": norm_gain, "out_weight": out_weight, "prev_feature": prev_feature, "draft_weight": draft_weight, "first_moment": first_moment, "second_moment": second_moment}


NEG_FILL = -1e+30
NORM_EPSILON = 1e-06
BETA_ONE = 0.9
BETA_TWO = 0.95
CORRECT_ONE = 1.0 - 0.9 ** 10
CORRECT_TWO = 1.0 - 0.95 ** 10
LEARN_RATE = 0.001

def ancestors(parents):
    node_count = parents.shape[-1]
    onehot = (parents[:, :, None] == jnp.arange(node_count, dtype=jnp.int32)[None, None, :]).astype(jnp.float32)
    reach_map = jnp.eye(node_count, dtype=jnp.float32)[None] + onehot
    for repeat in range(node_count.bit_length()):
        reach_map = jnp.minimum(jnp.einsum('rij,rjk->rik', reach_map, reach_map, precision=lax.Precision.HIGHEST), 1.0)
    return reach_map

def attend_one(operands):
    query_rows, cache_keys, cache_values, tree_keys, tree_values, length, visible = operands
    groups = HEADS // KV_HEADS
    score_scale = 1.0 / math.sqrt(HEAD)
    query_view = query_rows.astype(jnp.float32).reshape(NODES, KV_HEADS, groups, HEAD)
    cache_kview = cache_keys.astype(jnp.float32).reshape(CACHE, KV_HEADS, HEAD)
    cache_vview = cache_values.astype(jnp.float32).reshape(CACHE, KV_HEADS, HEAD)
    tree_kview = tree_keys.astype(jnp.float32).reshape(NODES, KV_HEADS, HEAD)
    tree_vview = tree_values.astype(jnp.float32).reshape(NODES, KV_HEADS, HEAD)
    cache_scores = jnp.einsum('nkgd,ckd->kgnc', query_view, cache_kview) * score_scale
    tree_scores = jnp.einsum('nkgd,jkd->kgnj', query_view, tree_kview) * score_scale
    cache_live = (jnp.arange(CACHE, dtype=jnp.int32) < length)[None, None, None, :]
    tree_live = (visible > 0.5)[None, None, :, :]
    cache_scores = jnp.where(cache_live, cache_scores, NEG_FILL)
    tree_scores = jnp.where(tree_live, tree_scores, NEG_FILL)
    row_top = jnp.maximum(lax.optimization_barrier(jnp.max(cache_scores, axis=-1)), lax.optimization_barrier(jnp.max(tree_scores, axis=-1)))
    cache_probs = jnp.where(cache_live, jnp.exp(cache_scores - row_top[..., None]), 0.0).astype(jnp.bfloat16)
    tree_probs = jnp.where(tree_live, jnp.exp(tree_scores - row_top[..., None]), 0.0).astype(jnp.bfloat16)
    totals = lax.optimization_barrier(jnp.sum(cache_probs.astype(jnp.float32), axis=-1)) + lax.optimization_barrier(jnp.sum(tree_probs.astype(jnp.float32), axis=-1))
    weighted = jnp.einsum('kgnc,ckd->nkgd', cache_probs.astype(jnp.float32), cache_vview)
    weighted = weighted + jnp.einsum('kgnj,jkd->nkgd', tree_probs.astype(jnp.float32), tree_vview)
    attended = (weighted / jnp.transpose(totals, (2, 0, 1))[..., None]).astype(jnp.bfloat16)
    return attended.reshape(NODES, HEADS * HEAD)

def reference(queries, cache_keys, cache_values, tree_keys, tree_values, parents, lengths, accepted_leaf, residual, norm_gain, out_weight, prev_feature, draft_weight, first_moment, second_moment):
    reach_map = ancestors(parents)
    attended = lax.map(attend_one, (queries, cache_keys, cache_values, tree_keys, tree_values, lengths, reach_map))
    row_count = REQS * NODES
    attended = attended.reshape(row_count, HEADS * HEAD)
    head_width = HEADS * HEAD // N_TP
    attn_parts = jnp.transpose(attended.reshape(row_count, N_TP, head_width), (1, 0, 2))
    weight_parts = out_weight.reshape(N_TP, head_width, D)

    def add_part(running, pair):
        piece_rows, piece_weight = pair
        term = jnp.dot(piece_rows, piece_weight, preferred_element_type=jnp.float32).astype(jnp.bfloat16)
        return (running + lax.optimization_barrier(term).astype(jnp.float32), None)
    projected, unused = lax.scan(add_part, jnp.zeros((row_count, D), jnp.float32), (attn_parts, weight_parts))
    mixed = residual.reshape(row_count, D).astype(jnp.float32) + projected
    mean_sq = lax.optimization_barrier(jnp.mean(mixed * mixed, axis=1, keepdims=True))
    features = (mixed * lax.rsqrt(mean_sq + NORM_EPSILON) * norm_gain[None, :]).astype(jnp.bfloat16)
    feature_table = jnp.concatenate([prev_feature[:, None, :], features.reshape(REQS, NODES, D)], axis=1)
    inputs = jnp.take_along_axis(feature_table, (parents + 1).astype(jnp.int32)[:, :, None], axis=1).reshape(row_count, D)
    leaf_hot = (accepted_leaf[:, None] == jnp.arange(NODES, dtype=jnp.int32)[None, :]).astype(jnp.float32)
    accepted = jnp.einsum('rn,rnj->rj', leaf_hot, reach_map, precision=lax.Precision.HIGHEST)
    fill_share = 0.5 + lengths.astype(jnp.float32) / CACHE
    weights = ((1.0 + 3.0 * accepted) * fill_share[:, None]).reshape(row_count, 1)
    predicted = jnp.dot(inputs, draft_weight, preferred_element_type=jnp.float32)
    pred_error = predicted - features.astype(jnp.float32)
    scaled_err = (weights * pred_error).astype(jnp.bfloat16)
    gradient = lax.dot_general(inputs, scaled_err, (((0,), (0,)), ((), ())), preferred_element_type=jnp.float32)
    draft_loss = 0.5 * jnp.sum(weights * pred_error * pred_error) / (row_count * D)
    grad_norm = jnp.sqrt(jnp.sum(gradient * gradient)) + 1e-06
    clip_factor = jnp.minimum(1.0, D / grad_norm)
    clipped = gradient * clip_factor
    new_first = BETA_ONE * first_moment + (1.0 - BETA_ONE) * clipped
    new_second = BETA_TWO * second_moment + (1.0 - BETA_TWO) * clipped * clipped
    direction = new_first / CORRECT_ONE / (jnp.sqrt(new_second / CORRECT_TWO) + 1e-08)
    new_weight = (draft_weight.astype(jnp.float32) - LEARN_RATE * direction).astype(jnp.bfloat16)
    return (features.reshape(REQS, NODES, D), new_weight, new_first, new_second, draft_loss)
```

```python
import functools
import math

import jax
import jax.numpy as jnp
from jax import lax
from jax.experimental import pallas as pl
from jax.experimental.pallas import tpu as pltpu
from jax.sharding import PartitionSpec as P

HEADS = 32
KV_HEADS = 4
HEAD = 128
NODES = 32
CACHE = 4096


NEG_FILL = -1e30
NORM_EPSILON = 1e-06
BETA_ONE = 0.9
BETA_TWO = 0.95
CORRECT_ONE = 1.0 - 0.9**10
CORRECT_TWO = 1.0 - 0.95**10
LEARN_RATE = 0.001


def closure(parents):
    node_count = parents.shape[-1]
    onehot = (parents[:, :, None] == jnp.arange(node_count, dtype=jnp.int32)[None, None, :]).astype(
        jnp.float32
    )
    reach_map = jnp.eye(node_count, dtype=jnp.float32)[None] + onehot
    for repeat in range(node_count.bit_length()):
        reach_map = jnp.minimum(
            jnp.einsum("rij,rjk->rik", reach_map, reach_map, precision=lax.Precision.HIGHEST), 1.0
        )
    return reach_map


VMEM = pl.BlockSpec(memory_space=pltpu.VMEM)
MESH = pl.DeviceIdType.MESH


def greet(axis, size):
    me = lax.axis_index(axis)
    barrier = pltpu.get_barrier_semaphore()
    for k in range(1, size):
        pl.semaphore_signal(
            barrier, inc=1, device_id={axis: lax.rem(me + k, size)}, device_id_type=MESH
        )
    pl.semaphore_wait(barrier, size - 1)


def params(cid):
    return pltpu.CompilerParams(
        collective_id=cid, has_side_effects=True, vmem_limit_bytes=40 * 1024 * 1024
    )


def exchange_kernel(axis, size, gather, count, *refs):
    ins, outs = refs[:count], refs[count : 2 * count]
    send_sem, recv_sem = refs[2 * count :]
    me = lax.axis_index(axis)
    greet(axis, size)
    copies = []
    for k in range(1, size):
        peer = lax.rem(me + k, size)
        for a in range(count):
            copy = pltpu.make_async_remote_copy(
                src_ref=ins[a] if gather else ins[a].at[peer],
                dst_ref=outs[a].at[me],
                send_sem=send_sem.at[a, k],
                recv_sem=recv_sem.at[a, k],
                device_id={axis: peer},
                device_id_type=MESH,
            )
            copy.start()
            copies.append(copy)
    for a in range(count):
        outs[a][me] = ins[a][...] if gather else ins[a][me]
    for copy in copies:
        copy.wait()


def exchange(arrays, axis, cid, gather=False):
    size = lax.axis_size(axis)
    count = len(arrays)
    shapes = [
        jax.ShapeDtypeStruct((size,) + a.shape if gather else a.shape, a.dtype) for a in arrays
    ]
    return pl.pallas_call(
        functools.partial(exchange_kernel, axis, size, gather, count),
        out_shape=shapes,
        in_specs=[VMEM] * count,
        out_specs=[VMEM] * count,
        scratch_shapes=[
            pltpu.SemaphoreType.DMA((count, size)),
            pltpu.SemaphoreType.DMA((count, size)),
        ],
        compiler_params=params(cid),
    )(*arrays)


def project_kernel(
    size, att, weight, residual, gain, out, parts, sent, squares, mine, mixed, sems
):
    me = lax.axis_index("tp")
    width = out.shape[1]
    model_width = width * size
    greet("tp", size)
    copies = []
    for k in range(1, size + 1):
        peer = lax.rem(me + k, size)
        columns = pl.ds(pl.multiple_of(peer * width, width), width)
        term = jnp.dot(att[...], weight[:, columns], preferred_element_type=jnp.float32)
        if k == size:
            parts[me] = term.astype(jnp.bfloat16)
        else:
            sent[peer] = term.astype(jnp.bfloat16)
            copy = pltpu.make_async_remote_copy(
                src_ref=sent.at[peer],
                dst_ref=parts.at[me],
                send_sem=sems.at[0, k],
                recv_sem=sems.at[1, k],
                device_id={"tp": peer},
                device_id_type=MESH,
            )
            copy.start()
            copies.append(copy)
    mixed[...] = residual[...].astype(jnp.float32) + parts[me].astype(jnp.float32)
    for k in range(1, size):
        copies[k - 1].wait()
        origin = lax.rem(me + size - k, size)
        mixed[...] += parts[origin].astype(jnp.float32)
    total = jnp.sum(mixed[...] * mixed[...], axis=1, keepdims=True)
    mine[...] = jnp.broadcast_to(total, mine.shape)
    copies = []
    for k in range(1, size):
        copy = pltpu.make_async_remote_copy(
            src_ref=mine,
            dst_ref=squares.at[me],
            send_sem=sems.at[2, k],
            recv_sem=sems.at[3, k],
            device_id={"tp": lax.rem(me + k, size)},
            device_id_type=MESH,
        )
        copy.start()
        copies.append(copy)
    squares[me] = mine[...]
    for copy in copies:
        copy.wait()
    total = jnp.sum(squares[...], axis=0)[:, 0:1] / model_width
    out[...] = (mixed[...] * lax.rsqrt(total + NORM_EPSILON) * gain[...]).astype(jnp.bfloat16)


def project(att, weight, residual, gain, cid):
    size = lax.axis_size("tp")
    rows, width = residual.shape
    return pl.pallas_call(
        functools.partial(project_kernel, size),
        out_shape=jax.ShapeDtypeStruct((rows, width), jnp.bfloat16),
        in_specs=[VMEM] * 4,
        out_specs=VMEM,
        scratch_shapes=[
            pltpu.VMEM((size, rows, width), jnp.bfloat16),
            pltpu.VMEM((size, rows, width), jnp.bfloat16),
            pltpu.VMEM((size, rows, 128), jnp.float32),
            pltpu.VMEM((rows, 128), jnp.float32),
            pltpu.VMEM((rows, width), jnp.float32),
            pltpu.SemaphoreType.DMA((4, size)),
        ],
        compiler_params=params(cid),
    )(att, weight, residual, gain)


def spread_kernel(reqs, tps, x_ref, out_ref, send_sem, recv_sem):
    per = tps // reqs
    r, t = lax.axis_index("req"), lax.axis_index("tp")
    goal, part = t // per, t % per
    own = r == goal
    barrier = pltpu.get_barrier_semaphore()

    def others(source, piece):
        return jnp.logical_or(r != source, t != r * per + piece)

    for source in range(reqs):
        for piece in range(per):

            @pl.when(others(source, piece))
            def _():
                pl.semaphore_signal(
                    barrier,
                    inc=1,
                    device_id={"req": source, "tp": r * per + piece},
                    device_id_type=MESH,
                )

    @pl.when(own)
    def _():
        pl.semaphore_wait(barrier, tps - 1)

    @pl.when(jnp.logical_not(own))
    def _():
        pl.semaphore_wait(barrier, tps)

    def send(k):
        return pltpu.make_async_remote_copy(
            src_ref=x_ref,
            dst_ref=out_ref.at[r, part],
            send_sem=send_sem.at[k],
            recv_sem=recv_sem.at[r * per + part],
            device_id={"req": goal, "tp": lax.rem(t + k, tps)},
            device_id_type=MESH,
        )

    for k in range(1, tps):
        send(k).start()

    @pl.when(jnp.logical_not(own))
    def _():
        send(0).start()

    @pl.when(own)
    def _():
        out_ref[r, part] = x_ref[...]

    for source in range(reqs):
        for piece in range(per):

            @pl.when(others(source, piece))
            def _():
                pltpu.make_async_remote_copy(
                    src_ref=x_ref,
                    dst_ref=out_ref.at[source, piece],
                    send_sem=send_sem.at[0],
                    recv_sem=recv_sem.at[source * per + piece],
                    device_id={"req": source, "tp": r * per + piece},
                    device_id_type=MESH,
                ).wait_recv()

    for k in range(1, tps):
        send(k).wait_send()

    @pl.when(jnp.logical_not(own))
    def _():
        send(0).wait_send()


def spread(x, cid):
    reqs, tps = lax.axis_size("req"), lax.axis_size("tp")
    return pl.pallas_call(
        functools.partial(spread_kernel, reqs, tps),
        out_shape=jax.ShapeDtypeStruct((reqs, tps // reqs) + x.shape, x.dtype),
        in_specs=[VMEM],
        out_specs=VMEM,
        scratch_shapes=[pltpu.SemaphoreType.DMA((tps,)), pltpu.SemaphoreType.DMA((tps,))],
        compiler_params=params(cid),
    )(x)


def body(
    queries,
    cache_keys,
    cache_values,
    tree_keys,
    tree_values,
    parents,
    lengths,
    accepted_leaf,
    residual,
    norm_gain,
    out_weight,
    prev_feature,
    draft_weight,
    first_moment,
    second_moment,
):
    requests = queries.shape[0]
    row_count = requests * NODES
    groups = HEADS // KV_HEADS
    score_scale = 1.0 / math.sqrt(HEAD)
    tps, reqs = lax.axis_size("tp"), lax.axis_size("req")
    tp_rank = lax.axis_index("tp")
    cache_span = cache_keys.shape[1]
    tree_span = tree_keys.shape[1]
    reach_map = closure(parents)
    query_view = queries.reshape(requests, NODES, KV_HEADS, groups, HEAD)
    cache_view = cache_keys.reshape(requests, cache_span, KV_HEADS, HEAD)
    tree_view = tree_keys.reshape(requests, tree_span, KV_HEADS, HEAD)
    cache_scores = (
        jnp.einsum("rnkgd,rckd->rkgnc", query_view, cache_view, preferred_element_type=jnp.float32)
        * score_scale
    )
    tree_scores = (
        jnp.einsum("rnkgd,rjkd->rkgnj", query_view, tree_view, preferred_element_type=jnp.float32)
        * score_scale
    )
    positions = tp_rank * cache_span + jnp.arange(cache_span, dtype=jnp.int32)
    cache_live = (positions[None, :] < lengths[:, None])[:, None, None, None, :]
    visible = lax.dynamic_slice_in_dim(reach_map, tp_rank * tree_span, tree_span, 2)
    tree_live = (visible > 0.5)[:, None, None, :, :]
    cache_scores = jnp.where(cache_live, cache_scores, NEG_FILL)
    tree_scores = jnp.where(tree_live, tree_scores, NEG_FILL)
    local_top = jnp.maximum(jnp.max(cache_scores, axis=-1), jnp.max(tree_scores, axis=-1))
    cache_probs = jnp.where(cache_live, jnp.exp(cache_scores - local_top[..., None]), 0.0).astype(
        jnp.bfloat16
    )
    tree_probs = jnp.where(tree_live, jnp.exp(tree_scores - local_top[..., None]), 0.0).astype(
        jnp.bfloat16
    )
    totals = jnp.sum(cache_probs, axis=-1, dtype=jnp.float32) + jnp.sum(
        tree_probs, axis=-1, dtype=jnp.float32
    )
    value_view = cache_values.reshape(requests, cache_span, KV_HEADS, HEAD)
    tree_value_view = tree_values.reshape(requests, tree_span, KV_HEADS, HEAD)
    weighted = jnp.einsum(
        "rkgnc,rckd->rkgnd", cache_probs, value_view, preferred_element_type=jnp.float32
    )
    weighted = weighted + jnp.einsum(
        "rkgnj,rjkd->rkgnd", tree_probs, tree_value_view, preferred_element_type=jnp.float32
    )
    own_heads = HEADS // tps
    weighted = weighted.astype(jnp.bfloat16).reshape(requests, tps, own_heads, NODES, HEAD)
    weighted = jnp.transpose(weighted, (1, 2, 0, 3, 4)).reshape(tps, own_heads * row_count, HEAD)

    def by_owner(x):
        x = x.reshape(requests, tps, own_heads, NODES)
        return jnp.transpose(x, (1, 2, 0, 3)).reshape(tps, own_heads, row_count)

    stats = jnp.concatenate([by_owner(local_top), by_owner(totals)], axis=1)
    weighted, stats = exchange([weighted, stats], "tp", 1)
    tops, totals = stats[:, :own_heads], stats[:, own_heads:]
    shares = jnp.exp(tops - jnp.max(tops, axis=0, keepdims=True))
    head_totals = jnp.sum(shares * totals, axis=0)
    shares = shares / head_totals[None]
    head_sums = jnp.sum(
        weighted.reshape(tps, own_heads, row_count, HEAD).astype(jnp.float32)
        * shares[:, :, :, None],
        axis=0,
    )
    attended = jnp.transpose(head_sums, (1, 0, 2)).reshape(row_count, own_heads * HEAD)
    attended = attended.astype(jnp.bfloat16)
    model_width = out_weight.shape[1]
    block_width = model_width // tps
    own_gain = lax.dynamic_slice_in_dim(norm_gain, tp_rank * block_width, block_width, 0)
    own_block = project(
        attended, out_weight, residual.reshape(row_count, block_width), own_gain[None, :], 2
    )
    own_prev = lax.dynamic_slice_in_dim(prev_feature, tp_rank * block_width, block_width, 1)
    node_hot = (parents[:, :, None] == jnp.arange(NODES, dtype=jnp.int32)[None, None, :]).astype(
        jnp.bfloat16
    )
    picked = jnp.einsum(
        "rij,rjd->rid",
        node_hot,
        own_block.reshape(requests, NODES, block_width),
        preferred_element_type=jnp.float32,
    )
    inputs = jnp.where(
        (parents < 0)[:, :, None], own_prev[:, None, :], picked.astype(jnp.bfloat16)
    ).reshape(row_count, block_width)
    leaf_hot = (accepted_leaf[:, None] == jnp.arange(NODES, dtype=jnp.int32)[None, :]).astype(
        jnp.float32
    )
    accepted = jnp.einsum("rn,rnj->rj", leaf_hot, reach_map, precision=lax.Precision.HIGHEST)
    fill_share = 0.5 + lengths.astype(jnp.float32) / CACHE
    weights = ((1.0 + 3.0 * accepted) * fill_share[:, None]).reshape(row_count, 1)
    all_inputs = spread(inputs, 3)
    per = tps // reqs
    all_inputs = [
        all_inputs[:, piece].reshape(reqs * row_count, block_width) for piece in range(per)
    ]
    terms = jnp.dot(
        all_inputs[0], draft_weight[:block_width], preferred_element_type=jnp.float32
    )
    for piece in range(1, per):
        terms = terms + jnp.dot(
            all_inputs[piece],
            draft_weight[piece * block_width : (piece + 1) * block_width],
            preferred_element_type=jnp.float32,
        )
    (terms,) = exchange(
        [terms.astype(jnp.bfloat16).reshape(reqs, row_count, block_width)], "req", 4
    )
    predicted = jnp.sum(terms.astype(jnp.float32), axis=0)
    pred_error = predicted - own_block.astype(jnp.float32)
    scaled_err = (weights * pred_error).astype(jnp.bfloat16)
    (all_err,) = exchange([scaled_err], "req", 5, gather=True)
    all_err = all_err.reshape(reqs * row_count, block_width)
    gradient = jnp.concatenate(
        [
            lax.dot_general(
                columns, all_err, (((0,), (0,)), ((), ())), preferred_element_type=jnp.float32
            )
            for columns in all_inputs
        ],
        axis=0,
    )
    sums = jnp.stack([jnp.sum(gradient * gradient), jnp.sum(weights * pred_error * pred_error)])
    sums = jnp.broadcast_to(jnp.repeat(sums, 4)[:, None], (8, 128))
    (sums,) = exchange([sums], "tp", 6, gather=True)
    (sums,) = exchange([jnp.sum(sums, axis=0)], "req", 7, gather=True)
    sums = jnp.sum(sums, axis=0)
    square_total, error_total = sums[0, 0], sums[4, 0]
    draft_loss = 0.5 * error_total / (row_count * reqs * model_width)
    grad_norm = jnp.sqrt(square_total) + 1e-06
    clip_factor = jnp.minimum(1.0, model_width / grad_norm)
    clipped = gradient * clip_factor
    new_first = BETA_ONE * first_moment + (1.0 - BETA_ONE) * clipped
    new_second = BETA_TWO * second_moment + (1.0 - BETA_TWO) * clipped * clipped
    direction = new_first / CORRECT_ONE / (jnp.sqrt(new_second / CORRECT_TWO) + 1e-08)
    new_weight = (draft_weight.astype(jnp.float32) - LEARN_RATE * direction).astype(jnp.bfloat16)
    return (
        own_block.reshape(requests, NODES, block_width),
        new_weight,
        new_first,
        new_second,
        draft_loss,
    )


def solution(mesh):
    placed = (
        P("req", None, None),
        P("req", "tp", None),
        P("req", "tp", None),
        P("req", "tp", None),
        P("req", "tp", None),
        P("req", None),
        P("req"),
        P("req"),
        P("req", None, "tp"),
        P(),
        P("tp", None),
        P("req", None),
        P("req", "tp"),
        P("req", "tp"),
        P("req", "tp"),
    )
    return jax.shard_map(
        body,
        mesh=mesh,
        in_specs=placed,
        out_specs=(P("req", None, "tp"), P("req", "tp"), P("req", "tp"), P("req", "tp"), P()),
        check_vma=False,
    )
```

```python
import functools
import math

import jax
import jax.numpy as jnp
from jax import lax
from jax.experimental import pallas as pl
from jax.experimental.pallas import tpu as pltpu
from jax.sharding import PartitionSpec as P

HEADS = 32
KV_HEADS = 4
HEAD = 128
NODES = 32
CACHE = 4096


NEG_FILL = -1e30
NORM_EPSILON = 1e-06
BETA_ONE = 0.9
BETA_TWO = 0.95
CORRECT_ONE = 1.0 - 0.9**10
CORRECT_TWO = 1.0 - 0.95**10
LEARN_RATE = 0.001


def closure(parents):
    node_count = parents.shape[-1]
    onehot = (parents[:, :, None] == jnp.arange(node_count, dtype=jnp.int32)[None, None, :]).astype(
        jnp.float32
    )
    reach_map = jnp.eye(node_count, dtype=jnp.float32)[None] + onehot
    for repeat in range(node_count.bit_length()):
        reach_map = jnp.minimum(
            jnp.einsum("rij,rjk->rik", reach_map, reach_map, precision=lax.Precision.HIGHEST), 1.0
        )
    return reach_map


VMEM = pl.BlockSpec(memory_space=pltpu.VMEM)
MESH = pl.DeviceIdType.MESH


def greet(axis, size):
    me = lax.axis_index(axis)
    barrier = pltpu.get_barrier_semaphore()
    for k in range(1, size):
        pl.semaphore_signal(
            barrier, inc=1, device_id={axis: lax.rem(me + k, size)}, device_id_type=MESH
        )
    pl.semaphore_wait(barrier, size - 1)


def params(cid):
    return pltpu.CompilerParams(
        collective_id=cid, has_side_effects=True, vmem_limit_bytes=40 * 1024 * 1024
    )


def exchange_kernel(axis, size, gather, count, *refs):
    ins, outs = refs[:count], refs[count : 2 * count]
    send_sem, recv_sem = refs[2 * count :]
    me = lax.axis_index(axis)
    greet(axis, size)
    copies = []
    for k in range(1, size):
        peer = lax.rem(me + k, size)
        for a in range(count):
            copy = pltpu.make_async_remote_copy(
                src_ref=ins[a] if gather else ins[a].at[peer],
                dst_ref=outs[a].at[me],
                send_sem=send_sem.at[a, k],
                recv_sem=recv_sem.at[a, k],
                device_id={axis: peer},
                device_id_type=MESH,
            )
            copy.start()
            copies.append(copy)
    for a in range(count):
        outs[a][me] = ins[a][...] if gather else ins[a][me]
    for copy in copies:
        copy.wait()


def exchange(arrays, axis, cid, gather=False):
    size = lax.axis_size(axis)
    count = len(arrays)
    shapes = [
        jax.ShapeDtypeStruct((size,) + a.shape if gather else a.shape, a.dtype) for a in arrays
    ]
    return pl.pallas_call(
        functools.partial(exchange_kernel, axis, size, gather, count),
        out_shape=shapes,
        in_specs=[VMEM] * count,
        out_specs=[VMEM] * count,
        scratch_shapes=[
            pltpu.SemaphoreType.DMA((count, size)),
            pltpu.SemaphoreType.DMA((count, size)),
        ],
        compiler_params=params(cid),
    )(*arrays)


def project_kernel(
    size, att, weight, residual, gain, out, parts, sent, sums, passed, squares, mine, mixed, near, far, small
):
    me = lax.axis_index("tp")
    width = out.shape[1]
    model_width = width * size
    zs, xs = 4, size // 4
    z, x = me // xs, me % xs
    greet("tp", size)

    def to_x(step, k):
        goal, other = lax.rem(z + step, zs), lax.rem(x + k, xs)
        return pltpu.make_async_remote_copy(
            src_ref=sent.at[goal, other],
            dst_ref=parts.at[goal, x],
            send_sem=near.at[0, step, k],
            recv_sem=near.at[1, step, k],
            device_id={"tp": z * xs + other},
            device_id_type=MESH,
        )

    def to_z(step):
        goal = lax.rem(z + step, zs)
        return pltpu.make_async_remote_copy(
            src_ref=passed.at[goal],
            dst_ref=sums.at[z],
            send_sem=far.at[0, step],
            recv_sem=far.at[1, step],
            device_id={"tp": goal * xs + x},
            device_id_type=MESH,
        )

    steps = [*range(1, zs), 0]
    for step in steps:
        goal = lax.rem(z + step, zs)
        for k in [*range(1, xs), 0]:
            other = lax.rem(x + k, xs)
            peer = goal * xs + other
            columns = pl.ds(pl.multiple_of(peer * width, width), width)
            term = jnp.dot(att[...], weight[:, columns], preferred_element_type=jnp.float32)
            term = term.astype(jnp.bfloat16)
            if k == 0:
                parts[goal, x] = term
            else:
                sent[goal, other] = term
                to_x(step, k).start()
    for step in steps:
        goal = lax.rem(z + step, zs)
        total = parts[goal, x].astype(jnp.float32)
        for k in range(1, xs):
            to_x(step, k).wait()
            total = total + parts[goal, lax.rem(x + xs - k, xs)].astype(jnp.float32)
        if step == 0:
            mixed[...] = residual[...].astype(jnp.float32) + total
        else:
            passed[goal] = total.astype(jnp.bfloat16)
            to_z(step).start()
    for step in range(1, zs):
        to_z(step).wait()
        mixed[...] += sums[lax.rem(z + zs - step, zs)].astype(jnp.float32)
    rows = mixed.shape[0]
    total = jnp.sum(mixed[...] * mixed[...], axis=1, keepdims=True)
    mine[...] = jnp.transpose(jnp.broadcast_to(total, (rows, 128)))[0:8]
    copies = []
    for k in range(1, size):
        copy = pltpu.make_async_remote_copy(
            src_ref=mine,
            dst_ref=squares.at[me],
            send_sem=small.at[0, k],
            recv_sem=small.at[1, k],
            device_id={"tp": lax.rem(me + k, size)},
            device_id_type=MESH,
        )
        copy.start()
        copies.append(copy)
    squares[me] = mine[...]
    for copy in copies:
        copy.wait()
    total = jnp.sum(squares[...], axis=0)[0:1]
    total = jnp.transpose(jnp.broadcast_to(total, (128, rows)))[:, 0:1] / model_width
    out[...] = (mixed[...] * lax.rsqrt(total + NORM_EPSILON) * gain[...]).astype(jnp.bfloat16)


def project(att, weight, residual, gain, cid):
    size = lax.axis_size("tp")
    rows, width = residual.shape
    return pl.pallas_call(
        functools.partial(project_kernel, size),
        out_shape=jax.ShapeDtypeStruct((rows, width), jnp.bfloat16),
        in_specs=[VMEM] * 4,
        out_specs=VMEM,
        scratch_shapes=[
            pltpu.VMEM((4, size // 4, rows, width), jnp.bfloat16),
            pltpu.VMEM((4, size // 4, rows, width), jnp.bfloat16),
            pltpu.VMEM((4, rows, width), jnp.bfloat16),
            pltpu.VMEM((4, rows, width), jnp.bfloat16),
            pltpu.VMEM((size, 8, rows), jnp.float32),
            pltpu.VMEM((8, rows), jnp.float32),
            pltpu.VMEM((rows, width), jnp.float32),
            pltpu.SemaphoreType.DMA((2, 4, size // 4)),
            pltpu.SemaphoreType.DMA((2, 4)),
            pltpu.SemaphoreType.DMA((2, size)),
        ],
        compiler_params=params(cid),
    )(att, weight, residual, gain)


def spread_kernel(reqs, tps, x_ref, out_ref, send_sem, recv_sem, pass_sem):
    per = tps // reqs
    zs, xs = 4, tps // 4
    r, t = lax.axis_index("req"), lax.axis_index("tp")
    z, x = t // xs, t % xs
    goal, part = t // per, t % per
    own = r == goal
    blocks = [(source, piece) for source in range(reqs) for piece in range(per)]
    barrier = pltpu.get_barrier_semaphore()

    def direct(piece):
        return (r * per + piece) % xs == x

    def others(source, piece):
        return jnp.logical_or(r != source, t != r * per + piece)

    for source, piece in blocks:

        @pl.when(jnp.logical_and(direct(piece), others(source, piece)))
        def _():
            pl.semaphore_signal(
                barrier,
                inc=1,
                device_id={"req": source, "tp": r * per + piece},
                device_id_type=MESH,
            )

    for k in range(1, xs):
        pl.semaphore_signal(
            barrier,
            inc=1,
            device_id={"req": r, "tp": z * xs + lax.rem(x + k, xs)},
            device_id_type=MESH,
        )

    @pl.when(own)
    def _():
        pl.semaphore_wait(barrier, zs + xs - 2)

    @pl.when(jnp.logical_not(own))
    def _():
        pl.semaphore_wait(barrier, zs + xs - 1)

    def send(k):
        return pltpu.make_async_remote_copy(
            src_ref=x_ref,
            dst_ref=out_ref.at[r, part],
            send_sem=send_sem.at[k],
            recv_sem=recv_sem.at[r * per + part],
            device_id={"req": goal, "tp": lax.rem(z + k, zs) * xs + x},
            device_id_type=MESH,
        )

    def forward(source, piece, k):
        return pltpu.make_async_remote_copy(
            src_ref=out_ref.at[source, piece],
            dst_ref=out_ref.at[source, piece],
            send_sem=pass_sem.at[source * per + piece, k],
            recv_sem=recv_sem.at[source * per + piece],
            device_id={"req": r, "tp": z * xs + lax.rem(x + k, xs)},
            device_id_type=MESH,
        )

    @pl.when(own)
    def _():
        out_ref[r, part] = x_ref[...]

    @pl.when(jnp.logical_not(own))
    def _():
        send(0).start()

    for k in range(1, zs):
        send(k).start()

    for source, piece in blocks:

        @pl.when(direct(piece))
        def _():
            @pl.when(others(source, piece))
            def _():
                forward(source, piece, 1).wait_recv()

            for k in range(1, xs):
                forward(source, piece, k).start()

    for source, piece in blocks:

        @pl.when(direct(piece))
        def _():
            for k in range(1, xs):
                forward(source, piece, k).wait_send()

        @pl.when(jnp.logical_not(direct(piece)))
        def _():
            forward(source, piece, 1).wait_recv()

    for k in range(1, zs):
        send(k).wait_send()

    @pl.when(jnp.logical_not(own))
    def _():
        send(0).wait_send()


def spread(x, cid):
    reqs, tps = lax.axis_size("req"), lax.axis_size("tp")
    return pl.pallas_call(
        functools.partial(spread_kernel, reqs, tps),
        out_shape=jax.ShapeDtypeStruct((reqs, tps // reqs) + x.shape, x.dtype),
        in_specs=[VMEM],
        out_specs=VMEM,
        scratch_shapes=[
            pltpu.SemaphoreType.DMA((4,)),
            pltpu.SemaphoreType.DMA((tps,)),
            pltpu.SemaphoreType.DMA((tps, tps // 4)),
        ],
        compiler_params=params(cid),
    )(x)


def body(
    queries,
    cache_keys,
    cache_values,
    tree_keys,
    tree_values,
    parents,
    lengths,
    accepted_leaf,
    residual,
    norm_gain,
    out_weight,
    prev_feature,
    draft_weight,
    first_moment,
    second_moment,
):
    requests = queries.shape[0]
    row_count = requests * NODES
    groups = HEADS // KV_HEADS
    score_scale = 1.0 / math.sqrt(HEAD)
    tps, reqs = lax.axis_size("tp"), lax.axis_size("req")
    tp_rank = lax.axis_index("tp")
    cache_span = cache_keys.shape[1]
    tree_span = tree_keys.shape[1]
    reach_map = closure(parents)
    query_view = queries.reshape(requests, NODES, KV_HEADS, groups, HEAD)
    cache_view = cache_keys.reshape(requests, cache_span, KV_HEADS, HEAD)
    tree_view = tree_keys.reshape(requests, tree_span, KV_HEADS, HEAD)
    cache_scores = (
        jnp.einsum("rnkgd,rckd->rkgnc", query_view, cache_view, preferred_element_type=jnp.float32)
        * score_scale
    )
    tree_scores = (
        jnp.einsum("rnkgd,rjkd->rkgnj", query_view, tree_view, preferred_element_type=jnp.float32)
        * score_scale
    )
    positions = tp_rank * cache_span + jnp.arange(cache_span, dtype=jnp.int32)
    cache_live = (positions[None, :] < lengths[:, None])[:, None, None, None, :]
    visible = lax.dynamic_slice_in_dim(reach_map, tp_rank * tree_span, tree_span, 2)
    tree_live = (visible > 0.5)[:, None, None, :, :]
    cache_scores = jnp.where(cache_live, cache_scores, NEG_FILL)
    tree_scores = jnp.where(tree_live, tree_scores, NEG_FILL)
    local_top = jnp.maximum(jnp.max(cache_scores, axis=-1), jnp.max(tree_scores, axis=-1))
    cache_probs = jnp.where(cache_live, jnp.exp(cache_scores - local_top[..., None]), 0.0).astype(
        jnp.bfloat16
    )
    tree_probs = jnp.where(tree_live, jnp.exp(tree_scores - local_top[..., None]), 0.0).astype(
        jnp.bfloat16
    )
    totals = jnp.sum(cache_probs, axis=-1, dtype=jnp.float32) + jnp.sum(
        tree_probs, axis=-1, dtype=jnp.float32
    )
    value_view = cache_values.reshape(requests, cache_span, KV_HEADS, HEAD)
    tree_value_view = tree_values.reshape(requests, tree_span, KV_HEADS, HEAD)
    weighted = jnp.einsum(
        "rkgnc,rckd->rkgnd", cache_probs, value_view, preferred_element_type=jnp.float32
    )
    weighted = weighted + jnp.einsum(
        "rkgnj,rjkd->rkgnd", tree_probs, tree_value_view, preferred_element_type=jnp.float32
    )
    own_heads = HEADS // tps
    weighted = weighted.astype(jnp.bfloat16).reshape(requests, tps, own_heads, NODES, HEAD)
    weighted = jnp.transpose(weighted, (1, 2, 0, 3, 4)).reshape(tps, own_heads * row_count, HEAD)

    def by_owner(x):
        x = x.reshape(requests, tps, own_heads, NODES)
        return jnp.transpose(x, (1, 2, 0, 3)).reshape(tps, own_heads, row_count)

    stats = jnp.concatenate([by_owner(local_top), by_owner(totals)], axis=1)
    weighted, stats = exchange([weighted, stats], "tp", 1)
    tops, totals = stats[:, :own_heads], stats[:, own_heads:]
    shares = jnp.exp(tops - jnp.max(tops, axis=0, keepdims=True))
    head_totals = jnp.sum(shares * totals, axis=0)
    shares = shares / head_totals[None]
    head_sums = jnp.sum(
        weighted.reshape(tps, own_heads, row_count, HEAD).astype(jnp.float32)
        * shares[:, :, :, None],
        axis=0,
    )
    attended = jnp.transpose(head_sums, (1, 0, 2)).reshape(row_count, own_heads * HEAD)
    attended = attended.astype(jnp.bfloat16)
    model_width = out_weight.shape[1]
    block_width = model_width // tps
    own_gain = lax.dynamic_slice_in_dim(norm_gain, tp_rank * block_width, block_width, 0)
    own_block = project(
        attended, out_weight, residual.reshape(row_count, block_width), own_gain[None, :], 2
    )
    own_prev = lax.dynamic_slice_in_dim(prev_feature, tp_rank * block_width, block_width, 1)
    node_hot = (parents[:, :, None] == jnp.arange(NODES, dtype=jnp.int32)[None, None, :]).astype(
        jnp.bfloat16
    )
    picked = jnp.einsum(
        "rij,rjd->rid",
        node_hot,
        own_block.reshape(requests, NODES, block_width),
        preferred_element_type=jnp.float32,
    )
    inputs = jnp.where(
        (parents < 0)[:, :, None], own_prev[:, None, :], picked.astype(jnp.bfloat16)
    ).reshape(row_count, block_width)
    leaf_hot = (accepted_leaf[:, None] == jnp.arange(NODES, dtype=jnp.int32)[None, :]).astype(
        jnp.float32
    )
    accepted = jnp.einsum("rn,rnj->rj", leaf_hot, reach_map, precision=lax.Precision.HIGHEST)
    fill_share = 0.5 + lengths.astype(jnp.float32) / CACHE
    weights = ((1.0 + 3.0 * accepted) * fill_share[:, None]).reshape(row_count, 1)
    all_inputs = spread(inputs, 3)
    per = tps // reqs
    all_inputs = [
        all_inputs[:, piece].reshape(reqs * row_count, block_width) for piece in range(per)
    ]
    terms = jnp.dot(
        all_inputs[0], draft_weight[:block_width], preferred_element_type=jnp.float32
    )
    for piece in range(1, per):
        terms = terms + jnp.dot(
            all_inputs[piece],
            draft_weight[piece * block_width : (piece + 1) * block_width],
            preferred_element_type=jnp.float32,
        )
    (terms,) = exchange(
        [terms.astype(jnp.bfloat16).reshape(reqs, row_count, block_width)], "req", 4
    )
    predicted = jnp.sum(terms.astype(jnp.float32), axis=0)
    pred_error = predicted - own_block.astype(jnp.float32)
    scaled_err = (weights * pred_error).astype(jnp.bfloat16)
    (all_err,) = exchange([scaled_err], "req", 5, gather=True)
    all_err = all_err.reshape(reqs * row_count, block_width)
    gradient = jnp.concatenate(
        [
            lax.dot_general(
                columns, all_err, (((0,), (0,)), ((), ())), preferred_element_type=jnp.float32
            )
            for columns in all_inputs
        ],
        axis=0,
    )
    sums = jnp.stack([jnp.sum(gradient * gradient), jnp.sum(weights * pred_error * pred_error)])
    sums = jnp.broadcast_to(jnp.repeat(sums, 4)[:, None], (8, 128))
    (sums,) = exchange([sums], "tp", 6, gather=True)
    (sums,) = exchange([jnp.sum(sums, axis=0)], "req", 7, gather=True)
    sums = jnp.sum(sums, axis=0)
    square_total, error_total = sums[0, 0], sums[4, 0]
    draft_loss = 0.5 * error_total / (row_count * reqs * model_width)
    grad_norm = jnp.sqrt(square_total) + 1e-06
    clip_factor = jnp.minimum(1.0, model_width / grad_norm)
    clipped = gradient * clip_factor
    new_first = BETA_ONE * first_moment + (1.0 - BETA_ONE) * clipped
    new_second = BETA_TWO * second_moment + (1.0 - BETA_TWO) * clipped * clipped
    direction = new_first / CORRECT_ONE / (jnp.sqrt(new_second / CORRECT_TWO) + 1e-08)
    new_weight = (draft_weight.astype(jnp.float32) - LEARN_RATE * direction).astype(jnp.bfloat16)
    return (
        own_block.reshape(requests, NODES, block_width),
        new_weight,
        new_first,
        new_second,
        draft_loss,
    )


def solution(mesh):
    placed = (
        P("req", None, None),
        P("req", "tp", None),
        P("req", "tp", None),
        P("req", "tp", None),
        P("req", "tp", None),
        P("req", None),
        P("req"),
        P("req"),
        P("req", None, "tp"),
        P(),
        P("tp", None),
        P("req", None),
        P("req", "tp"),
        P("req", "tp"),
        P("req", "tp"),
    )
    return jax.shard_map(
        body,
        mesh=mesh,
        in_specs=placed,
        out_specs=(P("req", None, "tp"), P("req", "tp"), P("req", "tp"), P("req", "tp"), P()),
        check_vma=False,
    )
```

```python
import functools
import math

import jax
import jax.numpy as jnp
from jax import lax
from jax.experimental import pallas as pl
from jax.experimental.pallas import tpu as pltpu
from jax.sharding import PartitionSpec as P

HEADS = 32
KV_HEADS = 4
HEAD = 128
NODES = 32
CACHE = 4096


NEG_FILL = -1e30
NORM_EPSILON = 1e-06
BETA_ONE = 0.9
BETA_TWO = 0.95
CORRECT_ONE = 1.0 - 0.9**10
CORRECT_TWO = 1.0 - 0.95**10
LEARN_RATE = 0.001


def closure(parents):
    node_count = parents.shape[-1]
    onehot = (parents[:, :, None] == jnp.arange(node_count, dtype=jnp.int32)[None, None, :]).astype(
        jnp.float32
    )
    reach_map = jnp.eye(node_count, dtype=jnp.float32)[None] + onehot
    for repeat in range(node_count.bit_length()):
        reach_map = jnp.minimum(
            jnp.einsum("rij,rjk->rik", reach_map, reach_map, precision=lax.Precision.HIGHEST), 1.0
        )
    return reach_map


VMEM = pl.BlockSpec(memory_space=pltpu.VMEM)
MESH = pl.DeviceIdType.MESH


def greet(axis, size):
    me = lax.axis_index(axis)
    barrier = pltpu.get_barrier_semaphore()
    for k in range(1, size):
        pl.semaphore_signal(
            barrier, inc=1, device_id={axis: lax.rem(me + k, size)}, device_id_type=MESH
        )
    pl.semaphore_wait(barrier, size - 1)


def params(cid):
    return pltpu.CompilerParams(
        collective_id=cid, has_side_effects=True, vmem_limit_bytes=40 * 1024 * 1024
    )


def exchange_kernel(axis, size, gather, count, *refs):
    ins, outs = refs[:count], refs[count : 2 * count]
    send_sem, recv_sem = refs[2 * count :]
    me = lax.axis_index(axis)
    greet(axis, size)
    copies = []
    for k in range(1, size):
        peer = lax.rem(me + k, size)
        for a in range(count):
            copy = pltpu.make_async_remote_copy(
                src_ref=ins[a] if gather else ins[a].at[peer],
                dst_ref=outs[a].at[me],
                send_sem=send_sem.at[a, k],
                recv_sem=recv_sem.at[a, k],
                device_id={axis: peer},
                device_id_type=MESH,
            )
            copy.start()
            copies.append(copy)
    for a in range(count):
        outs[a][me] = ins[a][...] if gather else ins[a][me]
    for copy in copies:
        copy.wait()


def exchange(arrays, axis, cid, gather=False):
    size = lax.axis_size(axis)
    count = len(arrays)
    shapes = [
        jax.ShapeDtypeStruct((size,) + a.shape if gather else a.shape, a.dtype) for a in arrays
    ]
    return pl.pallas_call(
        functools.partial(exchange_kernel, axis, size, gather, count),
        out_shape=shapes,
        in_specs=[VMEM] * count,
        out_specs=[VMEM] * count,
        scratch_shapes=[
            pltpu.SemaphoreType.DMA((count, size)),
            pltpu.SemaphoreType.DMA((count, size)),
        ],
        compiler_params=params(cid),
    )(*arrays)


def project_kernel(
    size, att, weight, residual, gain, out, parts, sent, sums, passed, squares, mine, mixed, near, far, small
):
    me = lax.axis_index("tp")
    width = out.shape[1]
    model_width = width * size
    zs, xs = 4, size // 4
    z, x = me // xs, me % xs
    greet("tp", size)

    def to_x(step, k):
        goal, other = lax.rem(z + step, zs), lax.rem(x + k, xs)
        return pltpu.make_async_remote_copy(
            src_ref=sent.at[goal, other],
            dst_ref=parts.at[goal, x],
            send_sem=near.at[0, step, k],
            recv_sem=near.at[1, step, k],
            device_id={"tp": z * xs + other},
            device_id_type=MESH,
        )

    def to_z(step):
        goal = lax.rem(z + step, zs)
        return pltpu.make_async_remote_copy(
            src_ref=passed.at[goal],
            dst_ref=sums.at[z],
            send_sem=far.at[0, step],
            recv_sem=far.at[1, step],
            device_id={"tp": goal * xs + x},
            device_id_type=MESH,
        )

    steps = [*range(1, zs), 0]
    for step in steps:
        goal = lax.rem(z + step, zs)
        for k in [*range(1, xs), 0]:
            other = lax.rem(x + k, xs)
            peer = goal * xs + other
            columns = pl.ds(pl.multiple_of(peer * width, width), width)
            term = jnp.dot(att[...], weight[:, columns], preferred_element_type=jnp.float32)
            term = term.astype(jnp.bfloat16)
            if k == 0:
                parts[goal, x] = term
            else:
                sent[goal, other] = term
                to_x(step, k).start()
    for step in steps:
        goal = lax.rem(z + step, zs)
        total = parts[goal, x].astype(jnp.float32)
        for k in range(1, xs):
            to_x(step, k).wait()
            total = total + parts[goal, lax.rem(x + xs - k, xs)].astype(jnp.float32)
        if step == 0:
            mixed[...] = residual[...].astype(jnp.float32) + total
        else:
            passed[goal] = total.astype(jnp.bfloat16)
            to_z(step).start()
    for step in range(1, zs):
        to_z(step).wait()
        mixed[...] += sums[lax.rem(z + zs - step, zs)].astype(jnp.float32)
    rows = mixed.shape[0]
    total = jnp.sum(mixed[...] * mixed[...], axis=1, keepdims=True)
    mine[...] = jnp.transpose(jnp.broadcast_to(total, (rows, 128)))[0:8]
    copies = []
    for k in range(1, size):
        copy = pltpu.make_async_remote_copy(
            src_ref=mine,
            dst_ref=squares.at[me],
            send_sem=small.at[0, k],
            recv_sem=small.at[1, k],
            device_id={"tp": lax.rem(me + k, size)},
            device_id_type=MESH,
        )
        copy.start()
        copies.append(copy)
    squares[me] = mine[...]
    for copy in copies:
        copy.wait()
    total = jnp.sum(squares[...], axis=0)[0:1]
    total = jnp.transpose(jnp.broadcast_to(total, (128, rows)))[:, 0:1] / model_width
    out[...] = (mixed[...] * lax.rsqrt(total + NORM_EPSILON) * gain[...]).astype(jnp.bfloat16)


def project(att, weight, residual, gain, cid):
    size = lax.axis_size("tp")
    rows, width = residual.shape
    return pl.pallas_call(
        functools.partial(project_kernel, size),
        out_shape=jax.ShapeDtypeStruct((rows, width), jnp.bfloat16),
        in_specs=[VMEM] * 4,
        out_specs=VMEM,
        scratch_shapes=[
            pltpu.VMEM((4, size // 4, rows, width), jnp.bfloat16),
            pltpu.VMEM((4, size // 4, rows, width), jnp.bfloat16),
            pltpu.VMEM((4, rows, width), jnp.bfloat16),
            pltpu.VMEM((4, rows, width), jnp.bfloat16),
            pltpu.VMEM((size, 8, rows), jnp.float32),
            pltpu.VMEM((8, rows), jnp.float32),
            pltpu.VMEM((rows, width), jnp.float32),
            pltpu.SemaphoreType.DMA((2, 4, size // 4)),
            pltpu.SemaphoreType.DMA((2, 4)),
            pltpu.SemaphoreType.DMA((2, size)),
        ],
        compiler_params=params(cid),
    )(att, weight, residual, gain)


def spread_kernel(reqs, tps, x_ref, out_ref, send_sem, recv_sem, pass_sem):
    per = tps // reqs
    zs, xs = 4, tps // 4
    r, t = lax.axis_index("req"), lax.axis_index("tp")
    z, x = t // xs, t % xs
    goal, part = t // per, t % per
    own = r == goal
    blocks = [(source, piece) for source in range(reqs) for piece in range(per)]
    barrier = pltpu.get_barrier_semaphore()

    def direct(piece):
        return (r * per + piece) % xs == x

    def others(source, piece):
        return jnp.logical_or(r != source, t != r * per + piece)

    for source, piece in blocks:

        @pl.when(jnp.logical_and(direct(piece), others(source, piece)))
        def _():
            pl.semaphore_signal(
                barrier,
                inc=1,
                device_id={"req": source, "tp": r * per + piece},
                device_id_type=MESH,
            )

    for k in range(1, xs):
        pl.semaphore_signal(
            barrier,
            inc=1,
            device_id={"req": r, "tp": z * xs + lax.rem(x + k, xs)},
            device_id_type=MESH,
        )

    @pl.when(own)
    def _():
        pl.semaphore_wait(barrier, zs + xs - 2)

    @pl.when(jnp.logical_not(own))
    def _():
        pl.semaphore_wait(barrier, zs + xs - 1)

    def send(k):
        return pltpu.make_async_remote_copy(
            src_ref=x_ref,
            dst_ref=out_ref.at[r, part],
            send_sem=send_sem.at[k],
            recv_sem=recv_sem.at[r * per + part],
            device_id={"req": goal, "tp": lax.rem(z + k, zs) * xs + x},
            device_id_type=MESH,
        )

    def forward(source, piece, k):
        return pltpu.make_async_remote_copy(
            src_ref=out_ref.at[source, piece],
            dst_ref=out_ref.at[source, piece],
            send_sem=pass_sem.at[source * per + piece, k],
            recv_sem=recv_sem.at[source * per + piece],
            device_id={"req": r, "tp": z * xs + lax.rem(x + k, xs)},
            device_id_type=MESH,
        )

    @pl.when(own)
    def _():
        out_ref[r, part] = x_ref[...]

    @pl.when(jnp.logical_not(own))
    def _():
        send(0).start()

    for k in range(1, zs):
        send(k).start()

    for source, piece in blocks:

        @pl.when(direct(piece))
        def _():
            @pl.when(others(source, piece))
            def _():
                forward(source, piece, 1).wait_recv()

            for k in range(1, xs):
                forward(source, piece, k).start()

    for source, piece in blocks:

        @pl.when(direct(piece))
        def _():
            for k in range(1, xs):
                forward(source, piece, k).wait_send()

        @pl.when(jnp.logical_not(direct(piece)))
        def _():
            forward(source, piece, 1).wait_recv()

    for k in range(1, zs):
        send(k).wait_send()

    @pl.when(jnp.logical_not(own))
    def _():
        send(0).wait_send()


def spread(x, cid):
    reqs, tps = lax.axis_size("req"), lax.axis_size("tp")
    return pl.pallas_call(
        functools.partial(spread_kernel, reqs, tps),
        out_shape=jax.ShapeDtypeStruct((reqs, tps // reqs) + x.shape, x.dtype),
        in_specs=[VMEM],
        out_specs=VMEM,
        scratch_shapes=[
            pltpu.SemaphoreType.DMA((4,)),
            pltpu.SemaphoreType.DMA((tps,)),
            pltpu.SemaphoreType.DMA((tps, tps // 4)),
        ],
        compiler_params=params(cid),
    )(x)


def settle_kernel(
    size, terms, features, weights, all_err, pred_error, parts, passed, sums, near, far, wide, last
):
    me = lax.axis_index("req")
    ys = size // 2
    y, c = me // 2, me % 2
    twin = y * 2 + 1 - c
    barrier = pltpu.get_barrier_semaphore()
    for peer in [twin] + [lax.rem(y + step, ys) * 2 + c for step in range(1, ys)]:
        pl.semaphore_signal(barrier, inc=1, device_id={"req": peer}, device_id_type=MESH)
    pl.semaphore_wait(barrier, ys)

    def copy(src, dst, sems, step, peer):
        return pltpu.make_async_remote_copy(
            src_ref=src,
            dst_ref=dst,
            send_sem=sems.at[0, step],
            recv_sem=sems.at[1, step],
            device_id={"req": peer},
            device_id_type=MESH,
        )

    def to_twin(step):
        goal = lax.rem(y + step, ys)
        return copy(terms.at[goal * 2 + 1 - c], parts.at[goal], near, step, twin)

    def to_y(step):
        goal = lax.rem(y + step, ys)
        return copy(passed.at[goal], sums.at[y], far, step, goal * 2 + c)

    def gather(step):
        return copy(all_err.at[me], all_err.at[me], wide, step, lax.rem(y + step, ys) * 2 + c)

    def forward(step):
        origin = lax.rem(y + ys - step, ys) * 2 + c
        return copy(all_err.at[origin], all_err.at[origin], last, step, twin)

    steps = [*range(1, ys), 0]
    for step in steps:
        to_twin(step).start()
    for step in steps:
        goal = lax.rem(y + step, ys)
        to_twin(step).wait()
        total = terms[goal * 2 + c].astype(jnp.float32) + parts[goal].astype(jnp.float32)
        if step == 0:
            pred_error[...] = total - features[...].astype(jnp.float32)
        else:
            passed[goal] = total.astype(jnp.bfloat16)
            to_y(step).start()
    for step in range(1, ys):
        to_y(step).wait()
        pred_error[...] += sums[lax.rem(y + ys - step, ys)].astype(jnp.float32)
    all_err[me] = (weights[...] * pred_error[...]).astype(jnp.bfloat16)
    for step in range(1, ys):
        gather(step).start()
    forward(0).start()
    for step in range(1, ys):
        gather(step).wait()
        forward(step).start()
    for step in range(ys):
        forward(step).wait()


def settle(terms, features, weights, cid):
    size, rows, width = terms.shape
    slots = pltpu.VMEM((size // 2, rows, width), jnp.bfloat16)
    return pl.pallas_call(
        functools.partial(settle_kernel, size),
        out_shape=[
            jax.ShapeDtypeStruct((size, rows, width), jnp.bfloat16),
            jax.ShapeDtypeStruct((rows, width), jnp.float32),
        ],
        in_specs=[VMEM] * 3,
        out_specs=[VMEM] * 2,
        scratch_shapes=[slots] * 3 + [pltpu.SemaphoreType.DMA((2, size // 2))] * 4,
        compiler_params=params(cid),
    )(terms, features, weights)


def body(
    queries,
    cache_keys,
    cache_values,
    tree_keys,
    tree_values,
    parents,
    lengths,
    accepted_leaf,
    residual,
    norm_gain,
    out_weight,
    prev_feature,
    draft_weight,
    first_moment,
    second_moment,
):
    requests = queries.shape[0]
    row_count = requests * NODES
    groups = HEADS // KV_HEADS
    score_scale = 1.0 / math.sqrt(HEAD)
    tps, reqs = lax.axis_size("tp"), lax.axis_size("req")
    tp_rank = lax.axis_index("tp")
    cache_span = cache_keys.shape[1]
    tree_span = tree_keys.shape[1]
    reach_map = closure(parents)
    query_view = queries.reshape(requests, NODES, KV_HEADS, groups, HEAD)
    cache_view = cache_keys.reshape(requests, cache_span, KV_HEADS, HEAD)
    tree_view = tree_keys.reshape(requests, tree_span, KV_HEADS, HEAD)
    cache_scores = (
        jnp.einsum("rnkgd,rckd->rkgnc", query_view, cache_view, preferred_element_type=jnp.float32)
        * score_scale
    )
    tree_scores = (
        jnp.einsum("rnkgd,rjkd->rkgnj", query_view, tree_view, preferred_element_type=jnp.float32)
        * score_scale
    )
    positions = tp_rank * cache_span + jnp.arange(cache_span, dtype=jnp.int32)
    cache_live = (positions[None, :] < lengths[:, None])[:, None, None, None, :]
    visible = lax.dynamic_slice_in_dim(reach_map, tp_rank * tree_span, tree_span, 2)
    tree_live = (visible > 0.5)[:, None, None, :, :]
    cache_scores = jnp.where(cache_live, cache_scores, NEG_FILL)
    tree_scores = jnp.where(tree_live, tree_scores, NEG_FILL)
    local_top = jnp.maximum(jnp.max(cache_scores, axis=-1), jnp.max(tree_scores, axis=-1))
    cache_probs = jnp.where(cache_live, jnp.exp(cache_scores - local_top[..., None]), 0.0).astype(
        jnp.bfloat16
    )
    tree_probs = jnp.where(tree_live, jnp.exp(tree_scores - local_top[..., None]), 0.0).astype(
        jnp.bfloat16
    )
    totals = jnp.sum(cache_probs, axis=-1, dtype=jnp.float32) + jnp.sum(
        tree_probs, axis=-1, dtype=jnp.float32
    )
    value_view = cache_values.reshape(requests, cache_span, KV_HEADS, HEAD)
    tree_value_view = tree_values.reshape(requests, tree_span, KV_HEADS, HEAD)
    weighted = jnp.einsum(
        "rkgnc,rckd->rkgnd", cache_probs, value_view, preferred_element_type=jnp.float32
    )
    weighted = weighted + jnp.einsum(
        "rkgnj,rjkd->rkgnd", tree_probs, tree_value_view, preferred_element_type=jnp.float32
    )
    own_heads = HEADS // tps
    weighted = weighted.astype(jnp.bfloat16).reshape(requests, tps, own_heads, NODES, HEAD)
    weighted = jnp.transpose(weighted, (1, 2, 0, 3, 4)).reshape(tps, own_heads * row_count, HEAD)

    def by_owner(x):
        x = x.reshape(requests, tps, own_heads, NODES)
        return jnp.transpose(x, (1, 2, 0, 3)).reshape(tps, own_heads, row_count)

    stats = jnp.concatenate([by_owner(local_top), by_owner(totals)], axis=1)
    weighted, stats = exchange([weighted, stats], "tp", 1)
    tops, totals = stats[:, :own_heads], stats[:, own_heads:]
    shares = jnp.exp(tops - jnp.max(tops, axis=0, keepdims=True))
    head_totals = jnp.sum(shares * totals, axis=0)
    shares = shares / head_totals[None]
    head_sums = jnp.sum(
        weighted.reshape(tps, own_heads, row_count, HEAD).astype(jnp.float32)
        * shares[:, :, :, None],
        axis=0,
    )
    attended = jnp.transpose(head_sums, (1, 0, 2)).reshape(row_count, own_heads * HEAD)
    attended = attended.astype(jnp.bfloat16)
    model_width = out_weight.shape[1]
    block_width = model_width // tps
    own_gain = lax.dynamic_slice_in_dim(norm_gain, tp_rank * block_width, block_width, 0)
    own_block = project(
        attended, out_weight, residual.reshape(row_count, block_width), own_gain[None, :], 2
    )
    own_prev = lax.dynamic_slice_in_dim(prev_feature, tp_rank * block_width, block_width, 1)
    node_hot = (parents[:, :, None] == jnp.arange(NODES, dtype=jnp.int32)[None, None, :]).astype(
        jnp.bfloat16
    )
    picked = jnp.einsum(
        "rij,rjd->rid",
        node_hot,
        own_block.reshape(requests, NODES, block_width),
        preferred_element_type=jnp.float32,
    )
    inputs = jnp.where(
        (parents < 0)[:, :, None], own_prev[:, None, :], picked.astype(jnp.bfloat16)
    ).reshape(row_count, block_width)
    leaf_hot = (accepted_leaf[:, None] == jnp.arange(NODES, dtype=jnp.int32)[None, :]).astype(
        jnp.float32
    )
    accepted = jnp.einsum("rn,rnj->rj", leaf_hot, reach_map, precision=lax.Precision.HIGHEST)
    fill_share = 0.5 + lengths.astype(jnp.float32) / CACHE
    weights = ((1.0 + 3.0 * accepted) * fill_share[:, None]).reshape(row_count, 1)
    all_inputs = spread(inputs, 3)
    per = tps // reqs
    all_inputs = [
        all_inputs[:, piece].reshape(reqs * row_count, block_width) for piece in range(per)
    ]
    terms = jnp.dot(
        all_inputs[0], draft_weight[:block_width], preferred_element_type=jnp.float32
    )
    for piece in range(1, per):
        terms = terms + jnp.dot(
            all_inputs[piece],
            draft_weight[piece * block_width : (piece + 1) * block_width],
            preferred_element_type=jnp.float32,
        )
    terms = terms.astype(jnp.bfloat16).reshape(reqs, row_count, block_width)
    all_err, pred_error = settle(terms, own_block, weights, 4)
    all_err = all_err.reshape(reqs * row_count, block_width)
    gradient = jnp.concatenate(
        [
            lax.dot_general(
                columns, all_err, (((0,), (0,)), ((), ())), preferred_element_type=jnp.float32
            )
            for columns in all_inputs
        ],
        axis=0,
    )
    sums = jnp.stack([jnp.sum(gradient * gradient), jnp.sum(weights * pred_error * pred_error)])
    sums = jnp.broadcast_to(jnp.repeat(sums, 4)[:, None], (8, 128))
    (sums,) = exchange([sums], "tp", 6, gather=True)
    (sums,) = exchange([jnp.sum(sums, axis=0)], "req", 7, gather=True)
    sums = jnp.sum(sums, axis=0)
    square_total, error_total = sums[0, 0], sums[4, 0]
    draft_loss = 0.5 * error_total / (row_count * reqs * model_width)
    grad_norm = jnp.sqrt(square_total) + 1e-06
    clip_factor = jnp.minimum(1.0, model_width / grad_norm)
    clipped = gradient * clip_factor
    new_first = BETA_ONE * first_moment + (1.0 - BETA_ONE) * clipped
    new_second = BETA_TWO * second_moment + (1.0 - BETA_TWO) * clipped * clipped
    direction = new_first / CORRECT_ONE / (jnp.sqrt(new_second / CORRECT_TWO) + 1e-08)
    new_weight = (draft_weight.astype(jnp.float32) - LEARN_RATE * direction).astype(jnp.bfloat16)
    return (
        own_block.reshape(requests, NODES, block_width),
        new_weight,
        new_first,
        new_second,
        draft_loss,
    )


def solution(mesh):
    placed = (
        P("req", None, None),
        P("req", "tp", None),
        P("req", "tp", None),
        P("req", "tp", None),
        P("req", "tp", None),
        P("req", None),
        P("req"),
        P("req"),
        P("req", None, "tp"),
        P(),
        P("tp", None),
        P("req", None),
        P("req", "tp"),
        P("req", "tp"),
        P("req", "tp"),
    )
    return jax.shard_map(
        body,
        mesh=mesh,
        in_specs=placed,
        out_specs=(P("req", None, "tp"), P("req", "tp"), P("req", "tp"), P("req", "tp"), P()),
        check_vma=False,
    )
```
